512 devices in a mesh: row: 32 (over x, z_hi, core), col: 16 (over y, z_lo).
Axes of the slice: x: 4, y: 4, z: 16 (z_hi: 4, z_lo: 4; z = z_hi * 4 + z_lo), core: 2. Of those that a mesh axis runs over, the one named last changes fastest.
Arguments:
- matrix: bfloat16 [16384, 16384], P('col', 'row'), may hold values from -2 to 2
- block_lists: int32 [16, 32, 16], replicated, may hold values from 0 to 32, as said below
Outputs:
- product: float32 [16384, 16384], P('col', 'row')
The draws below stay inside these ranges and needn't reach their ends.
Inputs may be any that keep to these rules, and one draw needn't show every extreme that they name: `block_lists`: each list holds distinct positions in ascending order, then 32 in unused entries; some device's list is full, and the block rows near one wall group are denser than the rest.
All inputs are finite; a program needn't handle non-finite values.
Results may differ from the reference program's by a relative error of at most 0.0003.
Values may be sent and summed in bfloat16 or wider, within the bound.
No kernel may reach another device: no remote copies, remote signals or barrier semaphores. Data moves between devices by JAX's collectives and lax.ppermute only.
A program may use at most 64 MiB of HBM per device.

```python
import jax
import jax.numpy as jnp
from jax import lax

BLOCK = 128
BCOLS = 4
BROWS = 8
NB = 128
ORDER = 16384
SLOTS = 32
MOST = 16
N_ROW = 32
N_COL = 16


def draw_block_lists(key, part):
    key = jax.random.fold_in(key, 7)
    key_order, key_sparse, key_dense, key_wall, key_full = jax.random.split(key, 5)
    device_count = N_COL * N_ROW
    orders = jax.vmap(lambda subkey: jax.random.permutation(subkey, SLOTS))(jax.random.split(key_order, device_count))
    lowest = max(1, SLOTS // 8)
    sparse_counts = jax.random.randint(key_sparse, (device_count,), lowest, MOST * 3 // 4 + 1)
    dense_counts = jax.random.randint(key_dense, (device_count,), MOST // 2, MOST + 1)
    wall_group = jax.random.randint(key_wall, (), 0, N_COL)
    group_of = jnp.arange(device_count) // N_ROW
    at_wall = (group_of == wall_group) | (group_of == (wall_group + 1) % N_COL)
    counts = jnp.where(at_wall, dense_counts, sparse_counts)
    chosen_row = jax.random.randint(key_full, (), 0, N_ROW)
    counts = jnp.where(jnp.arange(device_count) == wall_group * N_ROW + chosen_row, MOST, counts)
    position = jnp.arange(SLOTS)[None, :]
    chosen = jnp.where(position < counts[:, None], orders, SLOTS)
    chosen = jnp.sort(chosen, axis=1)[:, :MOST]
    return chosen.reshape(N_COL, N_ROW, MOST).astype(jnp.int32)


def steps_of(stream_key, extent, cuts, low, top_value):
    level = 1.0
    for axis_at, shards_of in cuts:
        draws = jax.random.uniform(jax.random.fold_in(jax.random.fold_in(stream_key, 6), axis_at), (shards_of,), jnp.float32, low / len(cuts), top_value / len(cuts))
        level = level * jnp.repeat(jnp.exp(draws), extent[axis_at] // shards_of).reshape((-1,) + (1,) * (len(extent) - 1 - axis_at))
    return level


def centred(stream_key, shape, spread, most, cuts=(), kind=jnp.bfloat16):
    values = jax.random.normal(stream_key, shape, jnp.float32) * spread
    if len(cuts) > 0:
        values = steps_of(stream_key, shape, cuts, -0.22, 0.18) * values
    return jnp.clip(values, min=-most, max=most).astype(kind)


def setup_inputs(seed: int = 0) -> dict:
    splits = jax.random.split(jax.random.key(seed), 3)
    matrix = centred(splits[0], (ORDER, ORDER), (1.0 / (2 * BROWS * BLOCK) ** 0.25), 2.0, ((0, 16), (1, 32)))
    block_lists = draw_block_lists(jax.random.fold_in(splits[2], 71), 0)
    return {"matrix": matrix, "block_lists": block_lists}


def occupied_rows(block_lists, group_index):
    entries = lax.dynamic_index_in_dim(block_lists, group_index, 0, keepdims=False)
    occupied = jnp.any(entries[:, :, None] == jnp.arange(SLOTS, dtype=jnp.int32)[None, None, :], axis=1)
    occupied = occupied.reshape(N_ROW, BROWS, BCOLS).transpose(1, 0, 2).reshape(BROWS, NB)
    return jnp.repeat(jnp.repeat(occupied, BLOCK, axis=0), BLOCK, axis=1)


def masked_rows(matrix, block_lists, group_index):
    height = BROWS * BLOCK
    offset = (group_index * height).astype(jnp.int32)
    row_slab = lax.dynamic_slice_in_dim(matrix, offset, height, 0).astype(jnp.float32)
    return jnp.where(occupied_rows(block_lists, group_index), row_slab, jnp.zeros_like(row_slab))


def reference(matrix, block_lists):
    height = BROWS * BLOCK

    def per_group(group_index):
        own_rows = masked_rows(matrix, block_lists, group_index)
        product = jnp.zeros((height, ORDER), jnp.float32)
        for fox_step in range(2):
            inner_group = ((group_index + fox_step) % N_COL).astype(jnp.int32)
            left_cols = lax.dynamic_slice_in_dim(own_rows, (inner_group * height).astype(jnp.int32), height, 1)
            right_rows = masked_rows(matrix, block_lists, inner_group)
            product = product + jnp.dot(left_cols, right_rows, precision=lax.Precision.HIGHEST, preferred_element_type=jnp.float32)
        return product

    stacked = lax.map(per_group, jnp.arange(N_COL, dtype=jnp.int32))
    return stacked.reshape(ORDER, ORDER)
```

```python
import functools

import jax
import jax.numpy as jnp
from jax import lax
from jax.experimental import pallas as pl
from jax.experimental.pallas import tpu as pltpu
from jax.sharding import PartitionSpec as P

BLOCK = 128
SLOTS = 32
MOST = 16
ROWS, COLS = 1024, 512
BCOLS = COLS // BLOCK
NX, NZ, NC = 4, 4, 2
N_ROW, N_COL = 32, 16
PART = MOST // NX

X_GROUPS = [[x * NZ * NC + i for x in range(NX)] for i in range(NZ * NC)]


def device(x, z, c, g):
    return ((x % NX * NZ + z % NZ) * NC + c) * N_COL + g


def z_moves(moves):
    return [
        (device(x, g + s, c, g), device(x, g + d, c, g))
        for g in range(N_COL)
        for s, d in moves
        for x in range(NX)
        for c in range(NC)
    ]


def pack_kernel(entries, piece, packed):
    for k in range(MOST):
        at = jnp.minimum(entries[k], SLOTS - 1)
        i, j = at // BCOLS, at % BCOLS
        packed[k] = piece[
            pl.ds(pl.multiple_of(i * BLOCK, BLOCK), BLOCK),
            pl.ds(pl.multiple_of(j * BLOCK, BLOCK), BLOCK),
        ]


def pack(matrix, entries):
    return pl.pallas_call(
        pack_kernel,
        out_shape=jax.ShapeDtypeStruct((MOST, BLOCK, BLOCK), matrix.dtype),
        grid_spec=pltpu.PrefetchScalarGridSpec(
            num_scalar_prefetch=1,
            grid=(1,),
            in_specs=[pl.BlockSpec((ROWS, COLS), lambda i, e: (0, 0))],
            out_specs=pl.BlockSpec((MOST, BLOCK, BLOCK), lambda i, e: (0, 0, 0)),
        ),
        compiler_params=pltpu.CompilerParams(vmem_limit_bytes=16 * 2**20),
    )(entries, matrix)


TILE = 256


def product_kernel(lists, left_a, left_b, right_a, right_b, out, left, right):
    core = lists[6, 0]

    @pl.when(pl.program_id(0) == 0)
    def _():
        left[...] = jnp.zeros_like(left)
        right[...] = jnp.zeros_like(right)

        def put_left(part, source, k, column):
            at = lists[column, k]
            i, j = at // BCOLS, at % BCOLS
            left[
                pl.ds(pl.multiple_of(i * BLOCK, BLOCK), BLOCK),
                pl.ds(pl.multiple_of(column * COLS + j * BLOCK, BLOCK), BLOCK),
            ] = source

        for k in range(MOST):
            for step in range(2):
                for ref, c in ((left_a, core), (left_b, 1 - core)):
                    put_left(step, ref[k // PART, step, k % PART], k, step * 2 + c)
        for step, ref in enumerate((right_a, right_b)):
            for k in range(MOST):
                at = lists[4 + step, k]
                i, j = at // BCOLS, at % BCOLS
                right[
                    step,
                    pl.ds(pl.multiple_of(i * BLOCK, BLOCK), BLOCK),
                    pl.ds(pl.multiple_of(j * BLOCK, BLOCK), BLOCK),
                ] = ref[k]

    rows = pl.ds(pl.multiple_of(pl.program_id(0) * TILE, TILE), TILE)
    out[...] = jnp.dot(
        left[rows, : 2 * COLS], right[0, :ROWS], preferred_element_type=jnp.float32
    ) + jnp.dot(
        left[rows, 2 * COLS :], right[1, :ROWS], preferred_element_type=jnp.float32
    )


def multiply(lists, left_a, left_b, right_a, right_b):
    whole = lambda *shape: pl.BlockSpec(shape, lambda i, e: (0,) * len(shape))
    half = (NX, 2, PART, BLOCK, BLOCK)
    piece = (MOST, BLOCK, BLOCK)
    return pl.pallas_call(
        product_kernel,
        out_shape=jax.ShapeDtypeStruct((ROWS, COLS), jnp.float32),
        grid_spec=pltpu.PrefetchScalarGridSpec(
            num_scalar_prefetch=1,
            grid=(ROWS // TILE,),
            in_specs=[whole(*half), whole(*half), whole(*piece), whole(*piece)],
            out_specs=pl.BlockSpec((TILE, COLS), lambda i, e: (i, 0)),
            scratch_shapes=[
                pltpu.VMEM((ROWS + BLOCK, 4 * COLS), jnp.bfloat16),
                pltpu.VMEM((2, ROWS + BLOCK, COLS), jnp.bfloat16),
            ],
        ),
        compiler_params=pltpu.CompilerParams(vmem_limit_bytes=32 * 2**20),
    )(lists, left_a, left_b, right_a, right_b)


def body(matrix, block_lists):
    g, h = lax.axis_index("col"), lax.axis_index("row")
    core, z = h % NC, h // NC % NZ
    at_row = (z - g) % NZ
    flat = block_lists.reshape(N_COL * N_ROW, MOST)
    g_next = (g + 1) % N_COL
    wanted = [g * N_ROW + (2 * g + j) % N_ROW for j in range(4)] + [
        g * N_ROW + h,
        g_next * N_ROW + h,
    ]
    lists = jnp.concatenate(
        [lax.dynamic_slice_in_dim(flat, w, 1, 0) for w in wanted]
        + [jnp.full((2, MOST), core, jnp.int32)]
    )

    own = pack(matrix, lists[4])
    both = ("row", "col")
    below = lax.ppermute(own, "col", [((i + 1) % N_COL, i) for i in range(N_COL)])
    spread = lax.all_to_all(own, "row", 0, 0, axis_index_groups=X_GROUPS, tiled=True)
    spread = spread.reshape(NX, PART, BLOCK, BLOCK)
    source_x = jnp.where(at_row == 1, g_next, g) // NZ
    unit = lax.dynamic_index_in_dim(spread, source_x, 0, keepdims=False)
    other = lax.ppermute(unit, both, z_moves([(0, 1), (1, 0)]))
    first = at_row == 0
    units = jnp.stack([jnp.where(first, unit, other), jnp.where(first, other, unit)])
    outer = lax.ppermute(units, both, z_moves([(0, 3), (1, 2)]))
    units = jnp.where(at_row < 2, units, outer)
    mine = lax.all_to_all(
        jnp.broadcast_to(units[None], (NX, *units.shape)),
        "row", 0, 0, axis_index_groups=X_GROUPS, tiled=True,
    )
    theirs = lax.ppermute(mine, "row", [(i, i ^ 1) for i in range(N_ROW)])
    return multiply(lists, mine, theirs, own, below)


def solution(mesh):
    return jax.shard_map(
        body,
        mesh=mesh,
        in_specs=(P("col", "row"), P()),
        out_specs=P("col", "row"),
        check_vma=False,
    )
```

```python
import jax
import jax.numpy as jnp
from jax import lax
from jax.experimental import pallas as pl
from jax.experimental.pallas import tpu as pltpu
from jax.sharding import PartitionSpec as P

BLOCK = 128
SLOTS = 32
MOST = 16
ROWS, COLS = 1024, 512
BCOLS = COLS // BLOCK
NX, NZ, NC = 4, 4, 2
N_ROW, N_COL = 32, 16
PART = MOST // NX
PIECE = (MOST, BLOCK, BLOCK)
TILE = 256
MIB = 2**20

X_GROUPS = [[x * NZ * NC + i for x in range(NX)] for i in range(NZ * NC)]


def device(x, z, c, g):
    return ((x % NX * NZ + z % NZ) * NC + c) * N_COL + g


def z_moves(moves):
    return [
        (device(x, g + s, c, g), device(x, g + d, c, g))
        for g in range(N_COL)
        for s, d in moves
        for x in range(NX)
        for c in range(NC)
    ]


def place(at):
    return (
        pl.ds(pl.multiple_of(at // BCOLS * BLOCK, BLOCK), BLOCK),
        pl.ds(pl.multiple_of(at % BCOLS * BLOCK, BLOCK), BLOCK),
    )


def pack_kernel(entries, piece, packed):
    for k in range(MOST):
        rows, cols = place(jnp.minimum(entries[k], SLOTS - 1))
        packed[k] = piece[rows, cols]


def pack(matrix, entries):
    return pl.pallas_call(
        pack_kernel,
        out_shape=jax.ShapeDtypeStruct(PIECE, matrix.dtype),
        grid_spec=pltpu.PrefetchScalarGridSpec(
            num_scalar_prefetch=1,
            grid=(1,),
            in_specs=[whole(ROWS, COLS)],
            out_specs=whole(*PIECE),
        ),
        compiler_params=pltpu.CompilerParams(vmem_limit_bytes=16 * MIB),
    )(entries, matrix)


def unpack(lists, which, source, dense):
    dense[...] = jnp.zeros(dense.shape, dense.dtype)
    for k in range(MOST):
        rows, cols = place(lists[which, k])
        dense[rows, cols] = source[k]


def tile_rows():
    return pl.ds(pl.multiple_of(pl.program_id(0) * TILE, TILE), TILE)


def partial_product(left, right, step, c, at):
    inner = pl.ds(pl.multiple_of(c * COLS, COLS), COLS)
    return jnp.dot(left[at], right[step, inner], preferred_element_type=jnp.float32)


def first_kernel(lists, mine, theirs, mine_later, own, below, out, right, left):
    core, flip = lists[6, 0], lists[6, 1]
    parts = ((mine, flip, core), (theirs, flip, 1 - core), (mine_later, 1 - flip, core))

    @pl.when(pl.program_id(0) == 0)
    def _():
        for i, (ref, step, c) in enumerate(parts):
            unpack(lists, step * 2 + c, ref, left.at[i])
        unpack(lists, 4, own, right.at[0])
        unpack(lists, 5, below, right.at[1])

    at = tile_rows()
    total = 0.0
    for i, (_, step, c) in enumerate(parts):
        total += partial_product(left.at[i], right, step, c, at)
    out[...] = total


def second_kernel(lists, theirs, right, partial, out, left):
    core, step = 1 - lists[6, 0], 1 - lists[6, 1]

    @pl.when(pl.program_id(0) == 0)
    def _():
        unpack(lists, step * 2 + core, theirs, left)

    out[...] = partial[...] + partial_product(left, right, step, core, tile_rows())


def whole(*shape):
    return pl.BlockSpec(shape, lambda i, e: (0,) * len(shape))


TILED = pl.BlockSpec((TILE, COLS), lambda i, e: (i, 0))
PRODUCT = jax.ShapeDtypeStruct((ROWS, COLS), jnp.float32)
DENSE = (ROWS + BLOCK, COLS)
RIGHT = jax.ShapeDtypeStruct((2, *DENSE), jnp.bfloat16)


def multiply_first(lists, mine, theirs, mine_later, own, below):
    return pl.pallas_call(
        first_kernel,
        out_shape=(PRODUCT, RIGHT),
        grid_spec=pltpu.PrefetchScalarGridSpec(
            num_scalar_prefetch=1,
            grid=(ROWS // TILE,),
            in_specs=[whole(*PIECE)] * 5,
            out_specs=(TILED, whole(2, *DENSE)),
            scratch_shapes=[pltpu.VMEM((3, *DENSE), jnp.bfloat16)],
        ),
        compiler_params=pltpu.CompilerParams(vmem_limit_bytes=24 * MIB),
        cost_estimate=pl.CostEstimate(flops=2 * ROWS * COLS * 1536, bytes_accessed=8 * MIB, transcendentals=0),
    )(lists, mine, theirs, mine_later, own, below)


def multiply_second(lists, theirs, right, partial):
    return pl.pallas_call(
        second_kernel,
        out_shape=PRODUCT,
        grid_spec=pltpu.PrefetchScalarGridSpec(
            num_scalar_prefetch=1,
            grid=(ROWS // TILE,),
            in_specs=[whole(*PIECE), whole(2, *DENSE), TILED],
            out_specs=TILED,
            scratch_shapes=[pltpu.VMEM(DENSE, jnp.bfloat16)],
        ),
        compiler_params=pltpu.CompilerParams(vmem_limit_bytes=24 * MIB),
    )(lists, theirs, right, partial)


def over_x(unit):
    return lax.all_to_all(
        jnp.broadcast_to(unit[None], (NX, *unit.shape)).reshape(PIECE),
        "row", 0, 0, axis_index_groups=X_GROUPS, tiled=True,
    )


def other_core(pieces):
    return lax.ppermute(pieces, "row", [(i, i ^ 1) for i in range(N_ROW)])


def body(matrix, block_lists):
    g, h = lax.axis_index("col"), lax.axis_index("row")
    core, z = h % NC, h // NC % NZ
    at_row = (z - g) % NZ
    g_next = (g + 1) % N_COL
    flip = ((at_row == 1) | (at_row == 2)).astype(jnp.int32)

    def entries(group, piece):
        return lax.dynamic_slice(block_lists, (group, piece, 0), (1, 1, MOST)).reshape(1, MOST)

    own_list = entries(g, h)
    lists = jnp.concatenate(
        [entries(g, (2 * g + j) % N_ROW) for j in range(4)]
        + [own_list, entries(g_next, h)]
        + [jnp.where(jnp.arange(MOST) == 0, core, flip).astype(jnp.int32)[None]]
    )
    own = pack(matrix, own_list.reshape(MOST))
    both = ("row", "col")
    spread = lax.all_to_all(own, "row", 0, 0, axis_index_groups=X_GROUPS, tiled=True)
    spread = spread.reshape(NX, PART, BLOCK, BLOCK)
    source_x = jnp.where(at_row == 1, g_next, g) // NZ
    unit = lax.dynamic_index_in_dim(spread, source_x, 0, keepdims=False)
    outer = lax.ppermute(unit, both, z_moves([(0, 3), (1, 2)]))
    unit = jnp.where(at_row < 2, unit, outer)
    other = lax.ppermute(unit, both, z_moves([(0, 1), (1, 0), (2, 3), (3, 2)]))
    own_late, unit = lax.optimization_barrier((own, unit))
    below = lax.ppermute(own_late, "col", [((i + 1) % N_COL, i) for i in range(N_COL)])
    mine = over_x(unit)
    theirs = other_core(mine)
    mine_later = over_x(other)
    mine_later, below = lax.optimization_barrier((mine_later, below))
    theirs_later = other_core(mine_later)
    partial, right = multiply_first(lists, mine, theirs, mine_later, own, below)
    return multiply_second(lists, theirs_later, right, partial)


def solution(mesh):
    return jax.shard_map(
        body,
        mesh=mesh,
        in_specs=(P("col", "row"), P()),
        out_specs=P("col", "row"),
        check_vma=False,
    )
```

```python
import jax
import jax.numpy as jnp
from jax import lax
from jax.experimental import pallas as pl
from jax.experimental.pallas import tpu as pltpu
from jax.sharding import PartitionSpec as P

BLOCK = 128
SLOTS = 32
MOST = 16
ROWS, COLS = 1024, 512
BCOLS = COLS // BLOCK
NX, NZ, NC = 4, 4, 2
N_ROW, N_COL = 32, 16
PART = MOST // NX
PIECE = (MOST, BLOCK, BLOCK)
TILE = 256
MIB = 2**20
VMEM = pl.BlockSpec(memory_space=pltpu.VMEM)

X_GROUPS = [[x * NZ * NC + i for x in range(NX)] for i in range(NZ * NC)]


def device(x, z, c, g):
    return ((x % NX * NZ + z % NZ) * NC + c) * N_COL + g


def x_moves(j):
    return [
        (device(k // NZ, k % NZ, c, g), device(k // NZ + j, k % NZ, c, g))
        for g in range(N_COL)
        for k in (g, (g + 1) % N_COL)
        for c in range(NC)
    ]


def z_moves(moves):
    return [
        (device(x, g + s, c, g), device(x, g + d, c, g))
        for g in range(N_COL)
        for s, d in moves
        for x in range(NX)
        for c in range(NC)
    ]


def place(at):
    return (
        pl.ds(pl.multiple_of(at // BCOLS * BLOCK, BLOCK), BLOCK),
        pl.ds(pl.multiple_of(at % BCOLS * BLOCK, BLOCK), BLOCK),
    )


def pack_kernel(entries, piece, packed):
    for k in range(MOST):
        source = (k + entries[MOST] * PART) % MOST
        rows, cols = place(jnp.minimum(entries[source], SLOTS - 1))
        packed[k // PART, k % PART] = piece[rows, cols]


def pack_quarters_kernel(entries, piece, *quarters):
    for k in range(MOST):
        source = (k + entries[MOST] * PART) % MOST
        rows, cols = place(jnp.minimum(entries[source], SLOTS - 1))
        quarters[k // PART][k % PART] = piece[rows, cols]


def pack(kernel, matrix, entries, shapes):
    return pl.pallas_call(
        kernel,
        out_shape=[jax.ShapeDtypeStruct(s, matrix.dtype) for s in shapes],
        in_specs=[pl.BlockSpec(memory_space=pltpu.SMEM), VMEM],
        out_specs=[VMEM] * len(shapes),
        compiler_params=pltpu.CompilerParams(vmem_limit_bytes=16 * MIB),
    )(entries, matrix)


def unpack(lists, which, source, dense):
    dense[...] = jnp.zeros(dense.shape, dense.dtype)
    for k in range(MOST):
        rows, cols = place(lists[which, k])
        dense[rows, cols] = source[k]


def inner(c):
    return pl.ds(pl.multiple_of(c * COLS, COLS), COLS)


def dense_left(lists, ref, left, c):
    for unit in range(2):
        step = unit ^ lists[6, 1]
        left[step] = jnp.zeros(left.shape[1:], left.dtype)
        for k in range(MOST):
            rows, cols = place(lists[step * 2 + c, k])
            left[step, rows, cols] = ref[k // PART, unit, k % PART]


def half_product(left, right, c, at):
    return jnp.dot(
        left[0, at], right[0, inner(c)], preferred_element_type=jnp.float32
    ) + jnp.dot(left[1, at], right[1, inner(c)], preferred_element_type=jnp.float32)


def first_kernel(lists, mine, own, below, out, right, left):
    core = lists[6, 0]
    dense_left(lists, mine, left, core)
    unpack(lists, 4, own, right.at[0])
    unpack(lists, 5, below, right.at[1])
    for t in range(0, ROWS, TILE):
        at = pl.ds(t, TILE)
        out[at] = half_product(left, right, core, at)


def second_kernel(lists, theirs, right, partial, out, left, done, sem):
    core = 1 - lists[6, 0]
    dense_left(lists, theirs, left, core)
    copies = []
    for i, t in enumerate(range(0, ROWS, TILE)):
        at = pl.ds(t, TILE)
        done[at] = partial[at] + half_product(left, right, core, at)
        copies.append(pltpu.make_async_copy(done.at[at], out.at[at], sem.at[i]))
        copies[-1].start()
    for copy in copies:
        copy.wait()


PRODUCT = jax.ShapeDtypeStruct((ROWS, COLS), jnp.float32)
DENSE = (ROWS + BLOCK, COLS)
RIGHT = jax.ShapeDtypeStruct((2, *DENSE), jnp.bfloat16)


def call(kernel, lists, operands, out_shape, out_specs, scratch, inner_size):
    return pl.pallas_call(
        kernel,
        out_shape=out_shape,
        in_specs=[pl.BlockSpec(memory_space=pltpu.SMEM)] + [VMEM] * len(operands),
        out_specs=out_specs,
        scratch_shapes=scratch,
        compiler_params=pltpu.CompilerParams(vmem_limit_bytes=8 * MIB),
        cost_estimate=pl.CostEstimate(
            flops=2 * ROWS * COLS * inner_size, bytes_accessed=8 * MIB, transcendentals=0
        ),
    )(lists, *operands)


def multiply_first(lists, *operands):
    scratch = [pltpu.VMEM((2, *DENSE), jnp.bfloat16)]
    return call(first_kernel, lists, operands, (PRODUCT, RIGHT), (VMEM, VMEM), scratch, 2 * COLS)


def multiply_second(lists, *operands):
    scratch = [
        pltpu.VMEM((2, *DENSE), jnp.bfloat16),
        pltpu.VMEM((ROWS, COLS), jnp.float32),
        pltpu.SemaphoreType.DMA((ROWS // TILE,)),
    ]
    anywhere = pl.BlockSpec(memory_space=pl.ANY)
    return call(second_kernel, lists, operands, PRODUCT, anywhere, scratch, 2 * COLS)


def over_x(unit):
    return lax.all_to_all(
        jnp.broadcast_to(unit[None], (NX, *unit.shape)),
        "row", 0, 0, axis_index_groups=X_GROUPS, tiled=True,
    )


def other_core(pieces):
    return lax.ppermute(pieces, "row", [(i, i ^ 1) for i in range(N_ROW)])


def body(matrix, block_lists):
    g, h = lax.axis_index("col"), lax.axis_index("row")
    core, z, x = h % NC, h // NC % NZ, h // NC // NZ
    at_row = (z - g) % NZ
    g_next = (g + 1) % N_COL
    flip = ((at_row == 1) | (at_row == 2)).astype(jnp.int32)

    def entries(group, piece):
        return lax.dynamic_slice(block_lists, (group, piece, 0), (1, 1, MOST)).reshape(1, MOST)

    own_list = entries(g, h)
    lists = jnp.concatenate(
        [entries(g, (2 * g + j) % N_ROW) for j in range(4)]
        + [own_list, entries(g_next, h)]
        + [jnp.where(jnp.arange(MOST) == 0, core, flip).astype(jnp.int32)[None]]
    )
    own_list = own_list.reshape(MOST)
    quarters = pack(
        pack_quarters_kernel, matrix, jnp.append(own_list, x.astype(jnp.int32)), [(PART, BLOCK, BLOCK)] * NX
    )
    own = pack(pack_kernel, matrix, jnp.append(own_list, 0), [(NX, PART, BLOCK, BLOCK)])[0]
    own = own.reshape(PIECE)
    both = ("row", "col")
    source = jnp.where(at_row == 1, g_next, g)
    is_source = (at_row < 2) & (x == source // NZ)
    unit = jnp.where(is_source, quarters[0], jnp.zeros_like(quarters[0]))
    for j in (2, 1, 3):
        unit = unit + lax.ppermute(quarters[j], both, x_moves(j))
    outer = lax.ppermute(unit, both, z_moves([(0, 3), (1, 2)]))
    below = lax.ppermute(own, "col", [((i + 1) % N_COL, i) for i in range(N_COL)])
    unit = jnp.where(at_row < 2, unit, outer)
    other = lax.ppermute(unit, both, z_moves([(0, 1), (1, 0), (2, 3), (3, 2)]))
    mine = over_x(jnp.stack([unit, other]))
    mine, below = lax.optimization_barrier((mine, below))
    theirs = other_core(mine)
    partial, right = multiply_first(lists, mine, own, below)
    return multiply_second(lists, theirs, right, partial)


def solution(mesh):
    return jax.shard_map(
        body,
        mesh=mesh,
        in_specs=(P("col", "row"), P()),
        out_specs=P("col", "row"),
        check_vma=False,
    )
```

```python
import jax
import jax.numpy as jnp
from jax import lax
from jax.experimental import pallas as pl
from jax.experimental.pallas import tpu as pltpu
from jax.sharding import PartitionSpec as P

BLOCK = 128
SLOTS = 32
MOST = 16
ROWS, COLS = 1024, 512
BCOLS = COLS // BLOCK
NX, NZ, NC = 4, 4, 2
N_ROW, N_COL = 32, 16
PART = MOST // NX
PIECE = (MOST, BLOCK, BLOCK)
TILE = 256
MIB = 2**20
VMEM = pl.BlockSpec(memory_space=pltpu.VMEM)

X_GROUPS = [[x * NZ * NC + i for x in range(NX)] for i in range(NZ * NC)]


def device(x, z, c, g):
    return ((x % NX * NZ + z % NZ) * NC + c) * N_COL + g


def x_moves(j):
    return [
        (device(k // NZ, k % NZ, c, g), device(k // NZ + j, k % NZ, c, g))
        for g in range(N_COL)
        for k in (g, (g + 1) % N_COL)
        for c in range(NC)
    ]


def z_moves(moves):
    return [
        (device(x, g + s, c, g), device(x, g + d, c, g))
        for g in range(N_COL)
        for s, d in moves
        for x in range(NX)
        for c in range(NC)
    ]


def place(at):
    return (
        pl.ds(pl.multiple_of(at // BCOLS * BLOCK, BLOCK), BLOCK),
        pl.ds(pl.multiple_of(at % BCOLS * BLOCK, BLOCK), BLOCK),
    )


def pack_kernel(lists, matrix, own, *rest):
    *quarters, entries, piece, list_sem, sem = rest
    g, h = lax.axis_index("col"), lax.axis_index("row")
    x = h // (NZ * NC)
    fetch = pltpu.make_async_copy(lists.at[g], entries, list_sem)
    fetch.start()
    loads = []
    for i in range(NX):
        rows = pl.ds(i * TILE, TILE)
        loads.append(pltpu.make_async_copy(matrix.at[rows], piece.at[rows], sem.at[i]))
        loads[-1].start()
    fetch.wait()
    for load in loads:
        load.wait()
    for k in range(MOST):
        rows, cols = place(jnp.minimum(entries[k, h], SLOTS - 1))
        own[k] = piece[rows, cols]
    for j, quarter in enumerate(quarters):
        first = (x + j) % NX * PART
        for k in range(PART):
            quarter[k] = own[first + k]


def pack(matrix, lists):
    anywhere = pl.BlockSpec(memory_space=pl.ANY)
    shapes = [PIECE] + [(PART, BLOCK, BLOCK)] * NX
    return pl.pallas_call(
        pack_kernel,
        out_shape=[jax.ShapeDtypeStruct(s, matrix.dtype) for s in shapes],
        in_specs=[anywhere, anywhere],
        out_specs=[VMEM] * len(shapes),
        scratch_shapes=[
            pltpu.SMEM((MOST, N_ROW), jnp.int32),
            pltpu.VMEM((ROWS, COLS), jnp.bfloat16),
            pltpu.SemaphoreType.DMA,
            pltpu.SemaphoreType.DMA((NX,)),
        ],
        compiler_params=pltpu.CompilerParams(vmem_limit_bytes=56 * MIB),
    )(lists, matrix)


def unpack(lists, which, source, dense):
    dense[...] = jnp.zeros(dense.shape, dense.dtype)
    for k in range(MOST):
        rows, cols = place(lists[which, k])
        dense[rows, cols] = source[k]


def inner(c):
    return pl.ds(pl.multiple_of(c * COLS, COLS), COLS)


def dense_left(lists, ref, left, c):
    for unit in range(2):
        step = unit ^ lists[6, 1]
        left[step] = jnp.zeros(left.shape[1:], left.dtype)
        for k in range(MOST):
            rows, cols = place(lists[step * 2 + c, k])
            left[step, rows, cols] = ref[k // PART, unit, k % PART]


def half_product(left, right, c, at):
    return jnp.dot(
        left[0, at], right[0, inner(c)], preferred_element_type=jnp.float32
    ) + jnp.dot(left[1, at], right[1, inner(c)], preferred_element_type=jnp.float32)


def first_kernel(lists, mine, own, below, out, right, left):
    core = lists[6, 0]
    dense_left(lists, mine, left, core)
    unpack(lists, 4, own, right.at[0])
    unpack(lists, 5, below, right.at[1])
    for t in range(0, ROWS, TILE):
        at = pl.ds(t, TILE)
        out[at] = half_product(left, right, core, at)


def second_kernel(lists, theirs, right, partial, out, left, done, sem):
    core = 1 - lists[6, 0]
    dense_left(lists, theirs, left, core)
    copies = []
    for i, t in enumerate(range(0, ROWS, TILE)):
        at = pl.ds(t, TILE)
        done[at] = partial[at] + half_product(left, right, core, at)
        copies.append(pltpu.make_async_copy(done.at[at], out.at[at], sem.at[i]))
        copies[-1].start()
    for copy in copies:
        copy.wait()


PRODUCT = jax.ShapeDtypeStruct((ROWS, COLS), jnp.float32)
DENSE = (ROWS + BLOCK, COLS)
RIGHT = jax.ShapeDtypeStruct((2, *DENSE), jnp.bfloat16)


def call(kernel, lists, operands, out_shape, out_specs, scratch, inner_size):
    return pl.pallas_call(
        kernel,
        out_shape=out_shape,
        in_specs=[pl.BlockSpec(memory_space=pltpu.SMEM)] + [VMEM] * len(operands),
        out_specs=out_specs,
        scratch_shapes=scratch,
        compiler_params=pltpu.CompilerParams(vmem_limit_bytes=8 * MIB),
        cost_estimate=pl.CostEstimate(
            flops=2 * ROWS * COLS * inner_size, bytes_accessed=8 * MIB, transcendentals=0
        ),
    )(lists, *operands)


def multiply_first(lists, *operands):
    scratch = [pltpu.VMEM((2, *DENSE), jnp.bfloat16)]
    return call(first_kernel, lists, operands, (PRODUCT, RIGHT), (VMEM, VMEM), scratch, 2 * COLS)


def multiply_second(lists, *operands):
    scratch = [
        pltpu.VMEM((2, *DENSE), jnp.bfloat16),
        pltpu.VMEM((ROWS, COLS), jnp.float32),
        pltpu.SemaphoreType.DMA((ROWS // TILE,)),
    ]
    anywhere = pl.BlockSpec(memory_space=pl.ANY)
    return call(second_kernel, lists, operands, PRODUCT, anywhere, scratch, 2 * COLS)


def over_x(unit):
    return lax.all_to_all(
        jnp.broadcast_to(unit[None], (NX, *unit.shape)),
        "row", 0, 0, axis_index_groups=X_GROUPS, tiled=True,
    )


def other_core(pieces):
    return lax.ppermute(pieces, "row", [(i, i ^ 1) for i in range(N_ROW)])


def body(matrix, block_lists):
    g, h = lax.axis_index("col"), lax.axis_index("row")
    core, z, x = h % NC, h // NC % NZ, h // NC // NZ
    at_row = (z - g) % NZ
    g_next = (g + 1) % N_COL
    flip = ((at_row == 1) | (at_row == 2)).astype(jnp.int32)

    def entries(group, piece):
        return lax.dynamic_slice(block_lists, (group, piece, 0), (1, 1, MOST)).reshape(1, MOST)

    own, *quarters = pack(matrix, jnp.transpose(block_lists, (0, 2, 1)))
    both = ("row", "col")
    block_lists, own = lax.optimization_barrier((block_lists, own))
    lists = jnp.concatenate(
        [entries(g, (2 * g + j) % N_ROW) for j in range(4)]
        + [entries(g, h), entries(g_next, h)]
        + [jnp.where(jnp.arange(MOST) == 0, core, flip).astype(jnp.int32)[None]]
    )
    source = jnp.where(at_row == 1, g_next, g)
    is_source = (at_row < 2) & (x == source // NZ)
    unit = jnp.where(is_source, quarters[0], jnp.zeros_like(quarters[0]))
    for j in (1, 3, 2):
        unit = unit + lax.ppermute(quarters[j], both, x_moves(j))
    lists, unit = lax.optimization_barrier((lists, unit))
    outer = lax.ppermute(unit, both, z_moves([(0, 3), (1, 2)]))
    below = lax.ppermute(own, "col", [((i + 1) % N_COL, i) for i in range(N_COL)])
    unit = jnp.where(at_row < 2, unit, outer)
    other = lax.ppermute(unit, both, z_moves([(0, 1), (1, 0), (2, 3), (3, 2)]))
    mine = over_x(jnp.stack([unit, other]))
    mine, below = lax.optimization_barrier((mine, below))
    theirs = other_core(mine)
    partial, right = multiply_first(lists, mine, own, below)
    return multiply_second(lists, theirs, right, partial)


def solution(mesh):
    return jax.shard_map(
        body,
        mesh=mesh,
        in_specs=(P("col", "row"), P()),
        out_specs=P("col", "row"),
        check_vma=False,
    )
```

```python
import jax
import jax.numpy as jnp
from jax import lax
from jax.experimental import pallas as pl
from jax.experimental.pallas import tpu as pltpu
from jax.sharding import PartitionSpec as P

BLOCK = 128
SLOTS = 32
MOST = 16
ROWS, COLS = 1024, 512
BCOLS = COLS // BLOCK
NX, NZ, NC = 4, 4, 2
N_ROW, N_COL = 32, 16
PART = MOST // NX
PIECE = (MOST, BLOCK, BLOCK)
TILE = 256
MIB = 2**20
VMEM = pl.BlockSpec(memory_space=pltpu.VMEM)

X_GROUPS = [[x * NZ * NC + i for x in range(NX)] for i in range(NZ * NC)]


def device(x, z, c, g):
    return ((x % NX * NZ + z % NZ) * NC + c) * N_COL + g


def x_moves(j):
    return [
        (device(k // NZ, k % NZ, c, g), device(k // NZ + j, k % NZ, c, g))
        for g in range(N_COL)
        for k in (g, (g + 1) % N_COL)
        for c in range(NC)
    ]


def z_moves(moves):
    return [
        (device(x, g + s, c, g), device(x, g + d, c, g))
        for g in range(N_COL)
        for s, d in moves
        for x in range(NX)
        for c in range(NC)
    ]


def place(at):
    return (
        pl.ds(pl.multiple_of(at // BCOLS * BLOCK, BLOCK), BLOCK),
        pl.ds(pl.multiple_of(at % BCOLS * BLOCK, BLOCK), BLOCK),
    )


def pack_kernel(lists, matrix, own, *rest):
    *quarters, entries, piece, list_sem, sem = rest
    g, h = lax.axis_index("col"), lax.axis_index("row")
    x = h // (NZ * NC)
    fetch = pltpu.make_async_copy(lists.at[g], entries, list_sem)
    fetch.start()
    loads = []
    for i in range(NX):
        rows = pl.ds(i * TILE, TILE)
        loads.append(pltpu.make_async_copy(matrix.at[rows], piece.at[rows], sem.at[i]))
        loads[-1].start()
    fetch.wait()
    for load in loads:
        load.wait()
    for k in range(MOST):
        rows, cols = place(jnp.minimum(entries[k, h], SLOTS - 1))
        own[k] = piece[rows, cols]
    for j, quarter in enumerate(quarters):
        first = (x + j) % NX * PART
        for k in range(PART):
            quarter[k] = own[first + k]


def pack(matrix, lists):
    anywhere = pl.BlockSpec(memory_space=pl.ANY)
    shapes = [PIECE] + [(PART, BLOCK, BLOCK)] * NX
    return pl.pallas_call(
        pack_kernel,
        out_shape=[jax.ShapeDtypeStruct(s, matrix.dtype) for s in shapes],
        in_specs=[anywhere, anywhere],
        out_specs=[VMEM] * len(shapes),
        scratch_shapes=[
            pltpu.SMEM((MOST, N_ROW), jnp.int32),
            pltpu.VMEM((ROWS, COLS), jnp.bfloat16),
            pltpu.SemaphoreType.DMA,
            pltpu.SemaphoreType.DMA((NX,)),
        ],
        compiler_params=pltpu.CompilerParams(vmem_limit_bytes=56 * MIB),
    )(lists, matrix)


def unpack(lists, which, source, dense):
    dense[...] = jnp.zeros(dense.shape, dense.dtype)
    for k in range(MOST):
        rows, cols = place(lists[which, k])
        dense[rows, cols] = source[k]


def inner(c):
    return pl.ds(pl.multiple_of(c * COLS, COLS), COLS)


def dense_left(lists, ref, left, c):
    for unit in range(2):
        step = unit ^ lists[6, 1]
        left[step] = jnp.zeros(left.shape[1:], left.dtype)
        for k in range(MOST):
            rows, cols = place(lists[step * 2 + c, k])
            left[step, rows, cols] = ref[k // PART, unit, k % PART]


def half_product(left, right, c, at):
    return jnp.dot(
        left[0, at], right[0, inner(c)], preferred_element_type=jnp.float32
    ) + jnp.dot(left[1, at], right[1, inner(c)], preferred_element_type=jnp.float32)


def first_kernel(lists, mine, own, below, out, right, left):
    core = lists[6, 0]
    dense_left(lists, mine, left, core)
    unpack(lists, 4, own, right.at[0])
    unpack(lists, 5, below, right.at[1])
    for t in range(0, ROWS, TILE):
        at = pl.ds(t, TILE)
        out[at] = half_product(left, right, core, at)


def second_kernel(lists, theirs, right, partial, out, left, done, sem):
    core = 1 - lists[6, 0]
    dense_left(lists, theirs, left, core)
    copies = []
    for i, t in enumerate(range(0, ROWS, TILE)):
        at = pl.ds(t, TILE)
        done[at] = partial[at] + half_product(left, right, core, at)
        copies.append(pltpu.make_async_copy(done.at[at], out.at[at], sem.at[i]))
        copies[-1].start()
    for copy in copies:
        copy.wait()


PRODUCT = jax.ShapeDtypeStruct((ROWS, COLS), jnp.float32)
DENSE = (ROWS + BLOCK, COLS)
RIGHT = jax.ShapeDtypeStruct((2, *DENSE), jnp.bfloat16)


def call(kernel, lists, operands, out_shape, out_specs, scratch, inner_size):
    return pl.pallas_call(
        kernel,
        out_shape=out_shape,
        in_specs=[pl.BlockSpec(memory_space=pltpu.SMEM)] + [VMEM] * len(operands),
        out_specs=out_specs,
        scratch_shapes=scratch,
        compiler_params=pltpu.CompilerParams(vmem_limit_bytes=8 * MIB),
        cost_estimate=pl.CostEstimate(
            flops=2 * ROWS * COLS * inner_size, bytes_accessed=8 * MIB, transcendentals=0
        ),
    )(lists, *operands)


def multiply_first(lists, *operands):
    scratch = [pltpu.VMEM((2, *DENSE), jnp.bfloat16)]
    return call(first_kernel, lists, operands, (PRODUCT, RIGHT), (VMEM, VMEM), scratch, 2 * COLS)


def multiply_second(lists, *operands):
    scratch = [
        pltpu.VMEM((2, *DENSE), jnp.bfloat16),
        pltpu.VMEM((ROWS, COLS), jnp.float32),
        pltpu.SemaphoreType.DMA((ROWS // TILE,)),
    ]
    anywhere = pl.BlockSpec(memory_space=pl.ANY)
    return call(second_kernel, lists, operands, PRODUCT, anywhere, scratch, 2 * COLS)


def over_x(unit):
    return lax.all_to_all(
        jnp.broadcast_to(unit[None], (NX, *unit.shape)),
        "row", 0, 0, axis_index_groups=X_GROUPS, tiled=True,
    )


def other_core(pieces):
    return lax.ppermute(pieces, "row", [(i, i ^ 1) for i in range(N_ROW)])


def body(matrix, block_lists):
    g, h = lax.axis_index("col"), lax.axis_index("row")
    core, z, x = h % NC, h // NC % NZ, h // NC // NZ
    at_row = (z - g) % NZ
    g_next = (g + 1) % N_COL
    flip = ((at_row == 1) | (at_row == 2)).astype(jnp.int32)

    def entries(group, piece):
        return lax.dynamic_slice(block_lists, (group, piece, 0), (1, 1, MOST)).reshape(1, MOST)

    own, *quarters = pack(matrix, jnp.transpose(block_lists, (0, 2, 1)))
    both = ("row", "col")
    block_lists, own = lax.optimization_barrier((block_lists, own))
    lists = jnp.concatenate(
        [entries(g, (2 * g + j) % N_ROW) for j in range(4)]
        + [entries(g, h), entries(g_next, h)]
        + [jnp.where(jnp.arange(MOST) == 0, core, flip).astype(jnp.int32)[None]]
    )
    source = jnp.where(at_row == 1, g_next, g)
    is_source = (at_row < 2) & (x == source // NZ)
    unit = jnp.where(is_source, quarters[0], jnp.zeros_like(quarters[0]))
    for j in (1, 2, 3):
        unit = unit + lax.ppermute(quarters[j], both, x_moves(j))
    lists, unit = lax.optimization_barrier((lists, unit))
    outer = lax.ppermute(unit, both, z_moves([(0, 3), (1, 2)]))
    below = lax.ppermute(own, "col", [((i + 1) % N_COL, i) for i in range(N_COL)])
    unit = jnp.where(at_row < 2, unit, outer)
    other = lax.ppermute(unit, both, z_moves([(0, 1), (1, 0), (2, 3), (3, 2)]))
    mine = over_x(jnp.stack([unit, other]))
    mine, below = lax.optimization_barrier((mine, below))
    theirs = other_core(mine)
    partial, right = multiply_first(lists, mine, own, below)
    return multiply_second(lists, theirs, right, partial)


def solution(mesh):
    return jax.shard_map(
        body,
        mesh=mesh,
        in_specs=(P("col", "row"), P()),
        out_specs=P("col", "row"),
        check_vma=False,
    )
```
